128 devices in a mesh: frames: 8 (over z, y_hi), rows: 16 (over y_lo, x, core).
Axes of the slice: x: 4, y: 4 (y_hi: 2, y_lo: 2; y = y_hi * 2 + y_lo), z: 4, core: 2. Of those that a mesh axis runs over, the one named last changes fastest.
Arguments:
- query: bfloat16 [8, 128, 128, 1536], P('frames', 'rows'), as said below
- keys: bfloat16 [8, 128, 128, 1536], P('frames', 'rows'), as said below
- values: bfloat16 [8, 128, 128, 1536], P('frames', 'rows'), as said below
- key_offsets: int32 [8, 256, 16], P('frames', 'rows'), may hold values from -16 to 16, as said below
- key_counts: int32 [8, 256], P('frames', 'rows'), may hold values from 8 to 16
- gain_query: float32 [1536], replicated, may hold values from 0.25 to 6
- gain_key: float32 [1536], replicated, may hold values from 0.25 to 6
Outputs:
- mixed: bfloat16 [8, 128, 128, 1536], P('frames', 'rows')
The draws below stay inside these ranges and needn't reach their ends.
Inputs may be any that keep to these rules, and one draw needn't show every extreme that they name: `query`: entries are between -10.5 and 10.5. `keys`: entries are between -10.5 and 10.5. `values`: entries are between -9 and 9. `key_offsets`: slot 0 of every query block has offset 0; the other slots of a block hold distinct nonzero offsets.
All inputs are finite; a program needn't handle non-finite values.
Results may differ from the reference program's by a relative error of at most 0.0019.
The reference program's roundings to bfloat16 on the way count: a program that leaves them out, or rounds other values in their place, can miss the bound.
Values may be sent and summed in bfloat16 or wider, within the bound.
No kernel may reach another device: no remote copies, remote signals or barrier semaphores. Data moves between devices by JAX's collectives and lax.ppermute only.
A program may use at most 192 MiB of HBM per device.

```python
import jax
import jax.numpy as jnp
from jax import lax

COLS = 128
H = 12
DH = 128
BLOCK = 64
K_SEL = 16
HALO_ROWS = 8
C = 1536
FRAMES = 8
ROWS = 128
NBF = 256
RB = 16


def blended(common, own, share):
    return jnp.sqrt(share) * common + jnp.sqrt(1.0 - share) * own


def gain_levels(key):
    level = jnp.exp(jax.random.uniform(jax.random.fold_in(key, 31), (H, 1), jnp.float32, jnp.log(0.15), jnp.log(0.4)))
    shift = jax.random.uniform(jax.random.fold_in(key, 37), (H, DH), jnp.float32, -0.3, 0.3)
    return (level, shift)


def draw_query(key, part):
    key = jax.random.fold_in(key, 11)
    shape = (FRAMES, ROWS, COLS, H * DH)
    common = jax.random.normal(jax.random.fold_in(key, 1), (1, ROWS, COLS, H * DH), jnp.float32)
    own = jax.random.normal(jax.random.fold_in(key, 2), shape, jnp.float32)
    return (1.5 * jnp.clip(blended(common, own, 0.9), -6.0, 6.0)).astype(jnp.bfloat16)


def draw_keys(key, part):
    key = jax.random.fold_in(key, 13)
    shape = (FRAMES, ROWS, COLS, H * DH)
    common = jax.random.normal(jax.random.fold_in(key, 1), (1, ROWS, COLS, H * DH), jnp.float32)
    own = jax.random.normal(jax.random.fold_in(key, 2), shape, jnp.float32)
    return jnp.clip(blended(common, own, 0.9), -6.0, 6.0).astype(jnp.bfloat16)


def draw_values(key, part):
    key = jax.random.fold_in(key, 23)
    shape = (FRAMES, ROWS, COLS, H * DH)
    common = jax.random.normal(jax.random.fold_in(key, 1), (1, ROWS, COLS, H * DH), jnp.float32)
    own = jax.random.normal(jax.random.fold_in(key, 2), shape, jnp.float32)
    return (1.5 * jnp.clip(blended(common, own, 0.85), -6.0, 6.0)).astype(jnp.bfloat16)


def draw_key_offsets(key, part):
    key = jax.random.fold_in(key, 5)
    span = HALO_ROWS * COLS // BLOCK
    candidates = 2 * span
    shape = (FRAMES, NBF, candidates)
    ranks = jax.random.randint(key, shape, 0, 1 << 20) * candidates + lax.broadcasted_iota(jnp.int32, shape, 2)
    order = jnp.argsort(ranks, axis=-1)[..., :K_SEL - 1].astype(jnp.int32)
    picked = jnp.where(order < span, order - span, order - span + 1)
    own = jnp.zeros((FRAMES, NBF, 1), jnp.int32)
    return jnp.concatenate((own, picked), axis=-1)


def draw_key_counts(key, part):
    key = jax.random.fold_in(key, 7)
    drawn = jax.random.randint(key, (FRAMES, NBF), K_SEL // 2, K_SEL + 1)
    frame_index = lax.broadcasted_iota(jnp.int32, (FRAMES, NBF), 0)
    block_index = lax.broadcasted_iota(jnp.int32, (FRAMES, NBF), 1)
    return jnp.where((frame_index == 0) & (block_index == 0), K_SEL, drawn).astype(jnp.int32)


def draw_gain_query(key, part):
    level, shift = gain_levels(key)
    key = jax.random.fold_in(key, 17)
    jitter = jax.random.uniform(key, (H, DH), jnp.float32, -0.12, 0.12)
    result = jnp.sqrt(level) * jnp.exp(shift + jitter)
    return result.reshape(H * DH)


def draw_gain_key(key, part):
    level, shift = gain_levels(key)
    key = jax.random.fold_in(key, 19)
    jitter = jax.random.uniform(key, (H, DH), jnp.float32, -0.12, 0.12)
    result = jnp.sqrt(level) * jnp.exp(jitter - shift)
    return result.reshape(H * DH)


def setup_inputs(seed: int = 0) -> dict:
    streams_of = jax.random.split(jax.random.key(seed), 8)
    return {
        "query": draw_query(jax.random.fold_in(streams_of[7], 71), 0),
        "keys": draw_keys(jax.random.fold_in(streams_of[7], 71), 0),
        "values": draw_values(jax.random.fold_in(streams_of[7], 71), 0),
        "key_offsets": draw_key_offsets(jax.random.fold_in(streams_of[7], 71), 0),
        "key_counts": draw_key_counts(jax.random.fold_in(streams_of[7], 71), 0),
        "gain_query": draw_gain_query(jax.random.fold_in(streams_of[7], 71), 0),
        "gain_key": draw_gain_key(jax.random.fold_in(streams_of[7], 71), 0),
    }


EPSILON = 1e-06
blocks_per_step = 4

def blockwise(fn, sources, items):

    def one_frame(frame_pair):
        frame_sources, frame_items = frame_pair
        grouped = jax.tree.map(lambda a: a.reshape((a.shape[0] // blocks_per_step, blocks_per_step) + a.shape[1:]), frame_items)
        result = lax.map(lambda group: fn(frame_sources, group), grouped)
        return jax.tree.map(lambda a: a.reshape((-1,) + a.shape[2:]), result)
    return lax.map(one_frame, (sources, items))

def group_attention(sources, group):
    keys_padded, values_padded = sources
    query_group, index, live = group
    count = query_group.shape[0]
    channels = query_group.shape[2]
    heads = channels // DH
    slots = index.shape[1]
    chosen_keys = keys_padded[index].reshape(count, slots, BLOCK, heads, DH).astype(jnp.float32)
    chosen_values = values_padded[index].reshape(count, slots, BLOCK, heads, DH).astype(jnp.float32)
    split_query = query_group.reshape(count, BLOCK, heads, DH).astype(jnp.float32)
    scores = jnp.einsum('bqhd,bjkhd->bhqjk', split_query, chosen_keys) * DH ** (-0.5)
    scores = jnp.where(live[:, None, None, :, None], scores, -1e+30)
    maxima = lax.optimization_barrier(jnp.max(scores, axis=(3, 4), keepdims=True))
    expo = jnp.exp(scores - maxima)
    total = lax.optimization_barrier(jnp.sum(expo, axis=(3, 4)))
    weights = expo.astype(jnp.bfloat16).astype(jnp.float32)
    summed = jnp.einsum('bhqjk,bjkhd->bqhd', weights, chosen_values)
    result = summed / jnp.transpose(total, (0, 2, 1))[..., None]
    return result.astype(jnp.bfloat16).reshape(count, BLOCK, channels)

def normalize(tokens, gain):
    split = tokens.astype(jnp.float32).reshape(tokens.shape[:-1] + (tokens.shape[-1] // DH, DH))
    scale = lax.rsqrt(lax.optimization_barrier(jnp.mean(split * split, axis=-1, keepdims=True)) + EPSILON)
    return (split * scale * gain.reshape(-1, DH)).reshape(tokens.shape).astype(jnp.bfloat16)

def frame_attention(temporal_query, temporal_keys, temporal_values):
    frame_count, positions, channels = temporal_query.shape
    shape4 = (frame_count, positions, channels // DH, DH)
    split_query = temporal_query.reshape(shape4).astype(jnp.float32)
    split_keys = temporal_keys.reshape(shape4).astype(jnp.float32)
    split_values = temporal_values.reshape(shape4).astype(jnp.float32)
    scores = jnp.einsum('fphd,gphd->phfg', split_query, split_keys) * DH ** (-0.5)
    maxima = lax.optimization_barrier(jnp.max(scores, axis=-1, keepdims=True))
    expo = jnp.exp(scores - maxima)
    total = lax.optimization_barrier(jnp.sum(expo, axis=-1))
    weights = expo.astype(jnp.bfloat16).astype(jnp.float32)
    summed = jnp.einsum('phfg,gphd->fphd', weights, split_values)
    result = summed / jnp.transpose(total, (2, 0, 1))[..., None]
    return result.astype(jnp.bfloat16).reshape(frame_count, positions, channels)

def reference(query, keys, values, key_offsets, key_counts, gain_query, gain_key):
    rim = ((0, 0), (HALO_ROWS, HALO_ROWS), (0, 0), (0, 0))
    query_blocks = query.reshape(FRAMES, NBF, BLOCK, C)
    keys_padded = jnp.pad(keys, rim).reshape(FRAMES, -1, BLOCK, C)
    values_padded = jnp.pad(values, rim).reshape(FRAMES, -1, BLOCK, C)
    local = jnp.arange(NBF, dtype=jnp.int32)[None, :, None]
    target = local + key_offsets
    slot_number = jnp.arange(K_SEL, dtype=jnp.int32)[None, None, :]
    live = (target >= 0) & (target < NBF) & (slot_number < key_counts[:, :, None])
    index = (target + RB).astype(jnp.int32)
    spatial = blockwise(group_attention, (keys_padded, values_padded), (query_blocks, index, live))
    spatial = spatial.reshape(FRAMES, ROWS, COLS, C)

    def one_row(row_tokens):
        return frame_attention(normalize(row_tokens, gain_query), normalize(row_tokens, gain_key), row_tokens)
    temporal = lax.map(one_row, jnp.moveaxis(spatial, 1, 0))
    temporal = jnp.moveaxis(temporal, 0, 1)
    return (spatial.astype(jnp.float32) + temporal.astype(jnp.float32)).astype(jnp.bfloat16)
```

```python
import functools

import jax
import jax.numpy as jnp
from jax import lax
from jax.experimental import pallas as pl
from jax.experimental.pallas import tpu as pltpu
from jax.sharding import PartitionSpec as P

DH = 128
BLOCK = 64
SLOTS = 16
CHUNK = 4
GROUPS = (4, 4, 4)
EPSILON = 1e-06
SCALE2 = DH**-0.5 * 1.4426950408889634
POSITIONS = 32
F32 = jnp.float32
BF16 = jnp.bfloat16
VMEM_LIMIT = 50 * 1024 * 1024


def times_transposed(a, b):
    return lax.dot_general(a, b, (((1,), (1,)), ((), ())), preferred_element_type=F32)


def times(a, b):
    return jnp.dot(a, b, preferred_element_type=F32)


def spatial_kernel(
    index, bias, query, own_keys, own_values, before, after, out, key_buf, value_buf, scores, maxima, sem, *, column, width
):
    blocks = query.shape[0]
    copies = []
    for number, (source, target, part) in enumerate(
        (
            (before.at[0], key_buf, 0),
            (own_keys.at[:, :, pl.ds(column, width)], key_buf, 1),
            (after.at[0], key_buf, 2),
            (before.at[1], value_buf, 0),
            (own_values.at[:, :, pl.ds(column, width)], value_buf, 1),
            (after.at[1], value_buf, 2),
        )
    ):
        copies.append(pltpu.make_async_copy(source, target.at[pl.ds(part * blocks, blocks)], sem.at[number]))
    for copy in copies:
        copy.start()
    for copy in copies:
        copy.wait()
    pairs = width // (2 * DH)
    span = CHUNK * BLOCK
    zeros = jnp.zeros((BLOCK, DH), BF16)

    def chosen(buffer, block, chunk, channels):
        return jnp.concatenate(
            [buffer[index[block, CHUNK * chunk + t], :, channels] for t in range(CHUNK)], axis=0
        )

    def score(block, pair, slot):
        channels = pl.ds(pair * 2 * DH, 2 * DH)
        both = query[block, :, channels]
        stacked = jnp.concatenate(
            [
                jnp.concatenate([both[:, :DH], zeros], axis=1),
                jnp.concatenate([zeros, both[:, DH:]], axis=1),
            ],
            axis=0,
        )
        largest = None
        for chunk in range(SLOTS // CHUNK):
            place = pl.ds(chunk * span, span)
            part = times_transposed(stacked, chosen(key_buf, block, chunk, channels)) + bias[block, :, place]
            scores[slot, :, place] = part
            largest = part if largest is None else jnp.maximum(largest, part)
        largest = jnp.max(largest, axis=-1, keepdims=True)
        maxima[slot] = jnp.broadcast_to(largest, (2 * BLOCK, DH))

    def combine(block, pair, slot):
        channels = pl.ds(pair * 2 * DH, 2 * DH)
        largest = maxima[slot][:, :1]
        summed, total = None, None
        for chunk in range(SLOTS // CHUNK):
            expo = jnp.exp2((scores[slot, :, pl.ds(chunk * span, span)] - largest) * SCALE2)
            total = expo if total is None else total + expo
            part = times(expo.astype(BF16), chosen(value_buf, block, chunk, channels))
            summed = part if summed is None else summed + part
        inverse = 1.0 / jnp.sum(total, axis=-1, keepdims=True)
        out[block, :, pl.ds(pair * 2 * DH, DH)] = (summed[:BLOCK, :DH] * inverse[:BLOCK]).astype(BF16)
        out[block, :, pl.ds(pair * 2 * DH + DH, DH)] = (summed[BLOCK:, DH:] * inverse[BLOCK:]).astype(BF16)

    for pair in range(pairs):
        score(0, pair, pair)

    def two_blocks(step, carry):
        block = 2 * step
        later = jnp.minimum(block + 2, blocks - 1)
        for pair in range(pairs):
            score(block + 1, pair, pairs + pair)
            combine(block, pair, pair)
        for pair in range(pairs):
            score(later, pair, pair)
            combine(block + 1, pair, pairs + pair)
        return carry

    lax.fori_loop(0, blocks // 2, two_blocks, 0)


def spatial(index, bias, query, keys, values, before, after, first, width):
    blocks = query.shape[0]
    anywhere = pl.BlockSpec(memory_space=pl.ANY)
    pairs = width // (2 * DH)
    group = first * DH // width
    return pl.pallas_call(
        functools.partial(spatial_kernel, column=first * DH, width=width),
        out_shape=jax.ShapeDtypeStruct((blocks, BLOCK, width), BF16),
        grid=(1,),
        in_specs=[
            pl.BlockSpec(memory_space=pltpu.SMEM),
            pl.BlockSpec(bias.shape, lambda i: (0, 0, 0)),
            pl.BlockSpec((blocks, BLOCK, width), lambda i: (0, 0, group)),
        ]
        + [anywhere] * 4,
        out_specs=pl.BlockSpec((blocks, BLOCK, width), lambda i: (0, 0, 0)),
        scratch_shapes=[
            pltpu.VMEM((3 * blocks, BLOCK, width), BF16),
            pltpu.VMEM((3 * blocks, BLOCK, width), BF16),
            pltpu.VMEM((2 * pairs, 2 * BLOCK, SLOTS * BLOCK), F32),
            pltpu.VMEM((2 * pairs, 2 * BLOCK, DH), F32),
            pltpu.SemaphoreType.DMA((6,)),
        ],
        compiler_params=pltpu.CompilerParams(vmem_limit_bytes=VMEM_LIMIT),
    )(index, bias, query, keys, values, before, after)


def temporal_kernel(gain_query, gain_key, tokens, out, *, width):
    frames, positions = tokens.shape[0], tokens.shape[1]
    rows = frames * POSITIONS
    place = lax.broadcasted_iota(jnp.int32, (rows, rows), 0) % POSITIONS
    other = lax.broadcasted_iota(jnp.int32, (rows, rows), 1) % POSITIONS
    same = place == other

    def step(number, carry):
        where = pl.ds(number * POSITIONS, POSITIONS)
        for head in range(width // DH):
            channels = pl.ds(head * DH, DH)
            block = tokens[:, where, channels].reshape(rows, DH)
            wide = block.astype(F32)
            scaled = wide * lax.rsqrt(jnp.mean(wide * wide, axis=-1, keepdims=True) + EPSILON)
            normed_query = (scaled * gain_query[:, channels]).astype(BF16)
            normed_key = (scaled * gain_key[:, channels]).astype(BF16)
            scores = jnp.where(same, times_transposed(normed_query, normed_key), -1e30)
            largest = jnp.max(scores, axis=-1, keepdims=True)
            expo = jnp.exp2((scores - largest) * SCALE2)
            total = jnp.sum(expo, axis=-1, keepdims=True)
            result = (times(expo.astype(BF16), block) * (1.0 / total)).astype(BF16)
            mixed = (wide + result.astype(F32)).astype(BF16)
            out[:, where, channels] = mixed.reshape(frames, POSITIONS, DH)
        return carry

    lax.fori_loop(0, positions // POSITIONS, step, 0)


def temporal(gain_query, gain_key, tokens, first):
    width = tokens.shape[2]
    whole = pl.BlockSpec(tokens.shape, lambda i: (0, 0, 0))
    gain = pl.BlockSpec((1, width), lambda i: (0, first * DH // width))
    return pl.pallas_call(
        functools.partial(temporal_kernel, width=width),
        out_shape=jax.ShapeDtypeStruct(tokens.shape, BF16),
        grid=(1,),
        in_specs=[gain, gain, whole],
        out_specs=whole,
        compiler_params=pltpu.CompilerParams(vmem_limit_bytes=VMEM_LIMIT),
    )(gain_query, gain_key, tokens)


def body(query, keys, values, key_offsets, key_counts, gain_query, gain_key):
    frame_count, stripe_rows, columns, channels = query.shape
    tokens = stripe_rows * columns
    blocks = tokens // BLOCK
    stripes, frames = lax.axis_size("rows"), lax.axis_size("frames")
    local = jnp.arange(blocks, dtype=jnp.int32)[:, None]
    target = local + key_offsets[0]
    global_block = lax.axis_index("rows") * blocks + target
    slot = jnp.arange(SLOTS, dtype=jnp.int32)[None, :]
    live = (global_block >= 0) & (global_block < stripes * blocks) & (slot < key_counts[0][:, None])
    index = target + blocks
    bias = jnp.repeat(jnp.where(live, 0.0, -1e30).astype(F32), BLOCK, axis=1)[:, None, :]
    shape = (blocks, BLOCK, channels)
    query, keys, values = query.reshape(shape), keys.reshape(shape), values.reshape(shape)
    gain_query, gain_key = gain_query[None], gain_key[None]
    up = [(i, i + 1) for i in range(stripes - 1)]
    down = [(j, i) for i, j in up]

    firsts = [sum(GROUPS[:g]) for g in range(len(GROUPS))]
    halos = []
    for first, heads in zip(firsts, GROUPS):
        part = slice(first * DH, (first + heads) * DH)
        both = jnp.stack([keys[:, :, part], values[:, :, part]])
        halos.append((lax.ppermute(both, "rows", up), lax.ppermute(both, "rows", down)))
    outs = []
    for (before, after), first, heads in zip(halos, firsts, GROUPS):
        width = heads * DH
        own = spatial(index, bias, query, keys, values, before, after, first, width)
        moved = lax.all_to_all(
            own.reshape(frames, tokens // frames, width), "frames", split_axis=0, concat_axis=0, tiled=True
        )
        mixed = temporal(gain_query, gain_key, moved, first)
        back = lax.all_to_all(mixed, "frames", split_axis=0, concat_axis=0, tiled=True)
        outs.append(back.reshape(tokens, width))
    return jnp.concatenate(outs, axis=1).reshape(frame_count, stripe_rows, columns, channels)


def solution(mesh):
    placed = (
        P("frames", "rows", None, None),
        P("frames", "rows", None, None),
        P("frames", "rows", None, None),
        P("frames", "rows", None),
        P("frames", "rows"),
        P(),
        P(),
    )
    return jax.shard_map(
        body, mesh=mesh, in_specs=placed, out_specs=P("frames", "rows", None, None), check_vma=False
    )
```

```python
import functools

import jax
import jax.numpy as jnp
from jax import lax
from jax.experimental import pallas as pl
from jax.experimental.pallas import tpu as pltpu
from jax.sharding import PartitionSpec as P

DH = 128
BLOCK = 64
SLOTS = 16
CHUNK = 4
GROUPS = (((4, False),), ((4, False),), ((4, True),))
EXCHANGES = (("F0",), ("F1",), ("R0", "F2"), ("R1", "R2"))
KERNELS = ("F0", "F1", "R0", "F2", "R1", "R2")
EPSILON = 1e-06
SCALE2 = DH**-0.5 * 1.4426950408889634
POSITIONS = 32
F32 = jnp.float32
BF16 = jnp.bfloat16
VMEM_LIMIT = 50 * 1024 * 1024


def times_transposed(a, b):
    return lax.dot_general(a, b, (((1,), (1,)), ((), ())), preferred_element_type=F32)


def times(a, b):
    return jnp.dot(a, b, preferred_element_type=F32)


def spatial_kernel(
    index, bias, all_queries, own_keys, own_values, before, after, *rest, column, width, middle, aliased
):
    crossed = rest[:-9] if aliased else rest[:-8]
    out, query, key_buf, value_buf, scores, maxima, sem, value_sem = rest[-8:]
    blocks = query.shape[0]
    part = pl.ds(column, width)

    def fetch(source, target, place, semaphore):
        return pltpu.make_async_copy(source, target.at[pl.ds(place * blocks, blocks)], semaphore)

    def fetch_all(kind, own, target, semaphore, act):
        act(fetch(own.at[:, :, part], target, 1, semaphore.at[0]))
        if not crossed:
            act(fetch(before.at[kind], target, 0, semaphore.at[1]))
            act(fetch(after.at[kind], target, 2, semaphore.at[2]))
            return
        stripe = lax.axis_index("rows")
        for place, source, number in ((0, before, middle), (2, after, middle - 1)):

            @pl.when(stripe == number)
            def _():
                act(fetch(crossed[0].at[kind], target, place, semaphore.at[1 + place // 2]))

            @pl.when(stripe != number)
            def _():
                act(fetch(source.at[kind], target, place, semaphore.at[1 + place // 2]))

    ask = pltpu.make_async_copy(all_queries.at[:, :, part], query, sem.at[3])
    ask.start()
    fetch_all(0, own_keys, key_buf, sem, lambda copy: copy.start())
    fetch_all(1, own_values, value_buf, value_sem, lambda copy: copy.start())
    ask.wait()
    fetch_all(0, own_keys, key_buf, sem, lambda copy: copy.wait())
    pairs = width // (2 * DH)
    span = CHUNK * BLOCK
    zeros = jnp.zeros((BLOCK, DH), BF16)

    def chosen(buffer, block, chunk, channels):
        return jnp.concatenate(
            [buffer[index[block, CHUNK * chunk + t], :, channels] for t in range(CHUNK)], axis=0
        )

    def score(block, pair, slot):
        channels = pl.ds(pair * 2 * DH, 2 * DH)
        both = query[block, :, channels]
        stacked = jnp.concatenate(
            [
                jnp.concatenate([both[:, :DH], zeros], axis=1),
                jnp.concatenate([zeros, both[:, DH:]], axis=1),
            ],
            axis=0,
        )
        largest = None
        for chunk in range(SLOTS // CHUNK):
            place = pl.ds(chunk * span, span)
            part = times_transposed(stacked, chosen(key_buf, block, chunk, channels)) + bias[block, :, place]
            scores[slot, :, place] = part
            largest = part if largest is None else jnp.maximum(largest, part)
        largest = jnp.max(largest, axis=-1, keepdims=True)
        maxima[slot] = jnp.broadcast_to(largest, (2 * BLOCK, DH))

    def combine(block, pair, slot):
        channels = pl.ds(pair * 2 * DH, 2 * DH)
        largest = maxima[slot][:, :1]
        summed, total = None, None
        for chunk in range(SLOTS // CHUNK):
            expo = jnp.exp2((scores[slot, :, pl.ds(chunk * span, span)] - largest) * SCALE2)
            total = expo if total is None else total + expo
            part = times(expo.astype(BF16), chosen(value_buf, block, chunk, channels))
            summed = part if summed is None else summed + part
        inverse = 1.0 / jnp.sum(total, axis=-1, keepdims=True)
        out[block, :, pl.ds(pair * 2 * DH, DH)] = (summed[:BLOCK, :DH] * inverse[:BLOCK]).astype(BF16)
        out[block, :, pl.ds(pair * 2 * DH + DH, DH)] = (summed[BLOCK:, DH:] * inverse[BLOCK:]).astype(BF16)

    for pair in range(pairs):
        score(0, pair, pair)
    fetch_all(1, own_values, value_buf, value_sem, lambda copy: copy.wait())

    def two_blocks(step, carry):
        block = 2 * step
        later = jnp.minimum(block + 2, blocks - 1)
        for pair in range(pairs):
            score(block + 1, pair, pairs + pair)
            combine(block, pair, pair)
        for pair in range(pairs):
            score(later, pair, pair)
            combine(block + 1, pair, pairs + pair)
        return carry

    lax.fori_loop(0, blocks // 2, two_blocks, 0)


def spatial(index, bias, query, keys, values, halo, first, width, middle, into, total, offset):
    blocks = query.shape[0]
    anywhere = pl.BlockSpec(memory_space=pl.ANY)
    pairs = width // (2 * DH)
    extra = () if into is None else (into.reshape(blocks, BLOCK, total),)
    return pl.pallas_call(
        functools.partial(
            spatial_kernel, column=first * DH, width=width, middle=middle, aliased=into is not None
        ),
        out_shape=jax.ShapeDtypeStruct((blocks, BLOCK, total), BF16),
        grid=(1,),
        in_specs=[
            pl.BlockSpec(memory_space=pltpu.SMEM),
            pl.BlockSpec(bias.shape, lambda i: (0, 0, 0)),
        ]
        + [anywhere] * (3 + len(halo) + len(extra)),
        out_specs=pl.BlockSpec((blocks, BLOCK, width), lambda i: (0, 0, offset // width)),
        scratch_shapes=[
            pltpu.VMEM((blocks, BLOCK, width), BF16),
            pltpu.VMEM((3 * blocks, BLOCK, width), BF16),
            pltpu.VMEM((3 * blocks, BLOCK, width), BF16),
            pltpu.VMEM((2 * pairs, 2 * BLOCK, SLOTS * BLOCK), F32),
            pltpu.VMEM((2 * pairs, 2 * BLOCK, DH), F32),
            pltpu.SemaphoreType.DMA((4,)),
            pltpu.SemaphoreType.DMA((3,)),
        ],
        input_output_aliases={5 + len(halo): 0} if extra else {},
        compiler_params=pltpu.CompilerParams(vmem_limit_bytes=VMEM_LIMIT),
    )(index, bias, query, keys, values, *halo, *extra)


def pack_kernel(keys, values, out):
    out[0] = keys[...]
    out[1] = values[...]


def pack(keys, values, first, width):
    blocks = keys.shape[0]
    step = blocks // 4
    some = pl.BlockSpec((step, BLOCK, width), lambda i: (i, 0, first * DH // width))
    return pl.pallas_call(
        pack_kernel,
        out_shape=jax.ShapeDtypeStruct((2, blocks, BLOCK, width), BF16),
        grid=(blocks // step,),
        in_specs=[some, some],
        out_specs=pl.BlockSpec((2, step, BLOCK, width), lambda i: (0, i, 0, 0)),
    )(keys, values)


def temporal_kernel(gain_query, gain_key, tokens, *rest, first):
    out = rest[-1]
    frames, positions = tokens.shape[0], tokens.shape[1]
    rows = frames * POSITIONS
    place = lax.broadcasted_iota(jnp.int32, (rows, rows), 0) % POSITIONS
    other = lax.broadcasted_iota(jnp.int32, (rows, rows), 1) % POSITIONS
    same = place == other

    def step(number, carry):
        where = pl.ds(number * POSITIONS, POSITIONS)
        for head in range(out.shape[2] // DH):
            channels = pl.ds(head * DH, DH)
            gains = pl.ds((first + head) * DH, DH)
            block = tokens[:, where, channels].reshape(rows, DH)
            wide = block.astype(F32)
            scaled = wide * lax.rsqrt(jnp.mean(wide * wide, axis=-1, keepdims=True) + EPSILON)
            normed_query = (scaled * gain_query[:, gains]).astype(BF16)
            normed_key = (scaled * gain_key[:, gains]).astype(BF16)
            scores = jnp.where(same, times_transposed(normed_query, normed_key), -1e30)
            largest = jnp.max(scores, axis=-1, keepdims=True)
            expo = jnp.exp2((scores - largest) * SCALE2)
            total = jnp.sum(expo, axis=-1, keepdims=True)
            result = (times(expo.astype(BF16), block) * (1.0 / total)).astype(BF16)
            mixed = (wide + result.astype(F32)).astype(BF16)
            out[:, where, channels] = mixed.reshape(frames, POSITIONS, DH)
        return carry

    lax.fori_loop(0, positions // POSITIONS, step, 0)


def temporal(gain_query, gain_key, tokens, source, first, width, into, total, offset):
    shape = tokens.shape[:2]
    extra = () if into is None else (into.reshape(shape + (total,)),)
    gain = pl.BlockSpec(gain_key.shape, lambda i: (0, 0))
    return pl.pallas_call(
        functools.partial(temporal_kernel, first=first),
        out_shape=jax.ShapeDtypeStruct(shape + (total,), BF16),
        grid=(1,),
        in_specs=[gain, gain, pl.BlockSpec(shape + (width,), lambda i: (0, 0, source // width))]
        + [pl.BlockSpec(memory_space=pl.ANY)] * len(extra),
        out_specs=pl.BlockSpec(shape + (width,), lambda i: (0, 0, offset // width)),
        input_output_aliases={3: 0} if extra else {},
        compiler_params=pltpu.CompilerParams(vmem_limit_bytes=VMEM_LIMIT),
    )(gain_query, gain_key, tokens, *extra)


def body(query, keys, values, key_offsets, key_counts, gain_query, gain_key):
    frame_count, stripe_rows, columns, channels = query.shape
    tokens = stripe_rows * columns
    blocks = tokens // BLOCK
    stripes, frames = lax.axis_size("rows"), lax.axis_size("frames")
    local = jnp.arange(blocks, dtype=jnp.int32)[:, None]
    target = local + key_offsets[0]
    global_block = lax.axis_index("rows") * blocks + target
    slot = jnp.arange(SLOTS, dtype=jnp.int32)[None, :]
    live = (global_block >= 0) & (global_block < stripes * blocks) & (slot < key_counts[0][:, None])
    index = target + blocks
    bias = jnp.repeat(jnp.where(live, 0.0, -1e30).astype(F32), BLOCK, axis=1)[:, None, :]
    shape = (blocks, BLOCK, channels)
    query, keys, values = query.reshape(shape), keys.reshape(shape), values.reshape(shape)
    gain_query, gain_key = gain_query[None], gain_key[None]
    middle = stripes // 2
    up = [(i, i + 1) for i in range(stripes - 1)]
    down = [(j, i) for i, j in up]
    leave = [(middle - 1, stripes - 1), (middle, 0)]
    arrive = [(stripes - 1, middle), (0, middle - 1)]

    sizes = [sum(heads for heads, _ in group) for group in GROUPS]
    firsts = [sum(sizes[:g]) for g in range(len(GROUPS))]
    halos, leaving, packs = {}, {}, {}
    for g, group in enumerate(GROUPS):
        first = firsts[g]
        for p, (heads, goes_round) in enumerate(group):
            both = pack(keys, values, first, heads * DH)
            packs[g, p] = both
            if goes_round:
                leaving[g, p] = lax.ppermute(both, "rows", leave)
                halos[g, p] = (
                    lax.ppermute(both, "rows", [p for p in up if p[0] != middle - 1]),
                    lax.ppermute(both, "rows", [p for p in down if p[0] != middle]),
                )
            else:
                halos[g, p] = (lax.ppermute(both, "rows", up), lax.ppermute(both, "rows", down))
            first += heads

    def after(value, previous):
        return value if previous is None else lax.optimization_barrier((value, previous))[0]

    def second_hops(previous):
        made = []
        for key, relayed in leaving.items():
            made.append(lax.ppermute(after(relayed, previous), "rows", arrive))
            halos[key] += (made[-1],)
        leaving.clear()
        return tuple(made)

    places = {}
    for number, pieces in enumerate(EXCHANGES):
        offset = 0
        for piece in pieces:
            places[piece] = (number, offset)
            offset += sizes[int(piece[1])] * DH
    totals = [sum(sizes[int(piece[1])] for piece in pieces) * DH for pieces in EXCHANGES]
    filled = [None] * len(EXCHANGES)
    exchanged = [None] * len(EXCHANGES)
    missing = [len(pieces) for pieces in EXCHANGES]
    previous, arrived = tuple(packs.values()), None
    for piece in KERNELS:
        g = int(piece[1])
        number, offset = places[piece]
        total = totals[number]
        if piece[0] == "F":
            first = firsts[g]
            for p, (heads, _) in enumerate(GROUPS[g]):
                filled[number] = spatial(
                    after(index, previous), bias, query, keys, values, halos[g, p], first, heads * DH, middle,
                    filled[number], total, offset,
                )
                previous = filled[number]
                first += heads
                offset += heads * DH
                if leaving:
                    arrived = second_hops(previous)
        else:
            if arrived is not None:
                previous, arrived = (previous, arrived), None

            came, source = places["F" + piece[1]]
            filled[number] = temporal(
                after(gain_query, previous), gain_key, exchanged[came], source, firsts[g], sizes[g] * DH,
                filled[number], total, offset,
            )
            previous = filled[number]
        missing[number] -= 1
        if missing[number] == 0:
            value = filled[number].reshape(frames, tokens // frames, total)
            if number:
                value = after(value, exchanged[number - 1])
            exchanged[number] = lax.all_to_all(value, "frames", split_axis=0, concat_axis=0, tiled=True)
    outs = []
    for g, size in enumerate(sizes):
        number, offset = places["R" + str(g)]
        outs.append(exchanged[number][:, :, offset : offset + size * DH].reshape(tokens, size * DH))
    return jnp.concatenate(outs, axis=1).reshape(frame_count, stripe_rows, columns, channels)


def solution(mesh):
    placed = (
        P("frames", "rows", None, None),
        P("frames", "rows", None, None),
        P("frames", "rows", None, None),
        P("frames", "rows", None),
        P("frames", "rows"),
        P(),
        P(),
    )
    return jax.shard_map(
        body, mesh=mesh, in_specs=placed, out_specs=P("frames", "rows", None, None), check_vma=False
    )
```

```python
import functools

import jax
import jax.numpy as jnp
from jax import lax
from jax.experimental import pallas as pl
from jax.experimental.pallas import tpu as pltpu
from jax.sharding import PartitionSpec as P

DH = 128
BLOCK = 64
SLOTS = 16
CHUNK = 4
GROUPS = (((4, False),), ((4, False),), ((4, True),))
EXCHANGES = (("F0",), ("F1", "R0"), ("F2",), ("R1", "R2"))
KERNELS = ("F0", "F1", "R0", "F2", "R1", "R2")
HOP_AFTER, HOP_BEFORE = "F1", "R1"
EPSILON = 1e-06
SCALE2 = DH**-0.5 * 1.4426950408889634
POSITIONS = 32
F32 = jnp.float32
BF16 = jnp.bfloat16
UNROLL = 16
VMEM_LIMIT = 50 * 1024 * 1024


def times_transposed(a, b):
    return lax.dot_general(a, b, (((1,), (1,)), ((), ())), preferred_element_type=F32)


def times(a, b):
    return jnp.dot(a, b, preferred_element_type=F32)


def spatial_kernel(index, bias, queries, keys, values, before, after, *rest, first, offset, pairs, middle, crossing):
    crossed = rest[0] if crossing else None
    out, query, key_buf, value_buf, result, scores, maxima, sem, out_sem = rest[-9:]
    blocks = query.shape[1]
    span = CHUNK * BLOCK
    two = 2 * DH
    zeros = jnp.zeros((BLOCK, DH), BF16)

    def fetch(pair, act):
        here = pl.ds(pair * two, two)
        own = pl.ds(first * DH + pair * two, two)

        def one(source, target, number):
            act(pltpu.make_async_copy(source, target, sem.at[pair, number]))

        one(queries.at[:, :, own], query.at[pair], 0)
        for kind, (mine, target) in enumerate(((keys, key_buf), (values, value_buf))):
            one(mine.at[:, :, own], target.at[pair, pl.ds(blocks, blocks)], 1 + 3 * kind)
            for side, (source, number) in enumerate(((before, middle), (after, middle - 1))):
                place = target.at[pair, pl.ds(2 * side * blocks, blocks)]
                name = 2 + 3 * kind + side
                if not crossing:
                    one(source.at[kind, :, :, here], place, name)
                    continue
                stripe = lax.axis_index("rows")

                @pl.when(stripe == number)
                def _():
                    one(crossed.at[kind, :, :, here], place, name)

                @pl.when(stripe != number)
                def _():
                    one(source.at[kind, :, :, here], place, name)

    def chosen(buffer, pair, block, chunk):
        return jnp.concatenate([buffer[pair, index[block, CHUNK * chunk + t]] for t in range(CHUNK)], axis=0)

    def score(pair, block, slot):
        both = query[pair, block]
        stacked = jnp.concatenate(
            [
                jnp.concatenate([both[:, :DH], zeros], axis=1),
                jnp.concatenate([zeros, both[:, DH:]], axis=1),
            ],
            axis=0,
        )
        largest = None
        for chunk in range(SLOTS // CHUNK):
            place = pl.ds(chunk * span, span)
            part = times_transposed(stacked, chosen(key_buf, pair, block, chunk)) + bias[block, :, place]
            scores[slot, :, place] = part
            largest = part if largest is None else jnp.maximum(largest, part)
        largest = jnp.max(largest, axis=-1, keepdims=True)
        maxima[slot] = jnp.broadcast_to(largest, (2 * BLOCK, DH))

    def combine(pair, block, slot):
        largest = maxima[slot][:, :1]
        total, weights, picked = None, [], []
        for chunk in range(SLOTS // CHUNK):
            expo = jnp.exp2((scores[slot, :, pl.ds(chunk * span, span)] - largest) * SCALE2)
            total = expo if total is None else total + expo
            weights.append(expo.astype(BF16))
            picked.append(chosen(value_buf, pair, block, chunk))
        summed = times(jnp.concatenate(weights, axis=1), jnp.concatenate(picked, axis=0))
        inverse = 1.0 / jnp.sum(total, axis=-1, keepdims=True)
        result[pair, block, :, pl.ds(0, DH)] = (summed[:BLOCK, :DH] * inverse[:BLOCK]).astype(BF16)
        result[pair, block, :, pl.ds(DH, DH)] = (summed[BLOCK:, DH:] * inverse[BLOCK:]).astype(BF16)

    def leave(pair):
        place = pl.ds(offset + pair * two, two)
        return pltpu.make_async_copy(result.at[pair], out.at[:, :, place], out_sem.at[pair])

    for pair in range(pairs):
        fetch(pair, lambda copy: copy.start())
    for pair in range(pairs):
        fetch(pair, lambda copy: copy.wait())
        score(pair, 0, 0)

        def some_blocks(step, carry, pair=pair):
            for t in range(UNROLL):
                block = UNROLL * step + t
                score(pair, jnp.minimum(block + 1, blocks - 1), (t + 1) % 2)
                combine(pair, block, t % 2)
            return carry

        lax.fori_loop(0, blocks // UNROLL, some_blocks, 0)
        leave(pair).start()
    for pair in range(pairs):
        leave(pair).wait()


def spatial(index, bias, query, keys, values, halo, first, width, middle, into, total, offset):
    blocks = query.shape[0]
    anywhere = pl.BlockSpec(memory_space=pl.ANY)
    two = 2 * DH
    pairs = width // two
    extra = () if into is None else (into.reshape(blocks, BLOCK, total),)
    return pl.pallas_call(
        functools.partial(
            spatial_kernel, first=first, offset=offset, pairs=pairs, middle=middle, crossing=len(halo) == 3
        ),
        out_shape=jax.ShapeDtypeStruct((blocks, BLOCK, total), BF16),
        in_specs=[pl.BlockSpec(memory_space=pltpu.SMEM), pl.BlockSpec(memory_space=pltpu.VMEM)]
        + [anywhere] * (3 + len(halo) + len(extra)),
        out_specs=anywhere,
        scratch_shapes=[
            pltpu.VMEM((pairs, blocks, BLOCK, two), BF16),
            pltpu.VMEM((pairs, 3 * blocks, BLOCK, two), BF16),
            pltpu.VMEM((pairs, 3 * blocks, BLOCK, two), BF16),
            pltpu.VMEM((pairs, blocks, BLOCK, two), BF16),
            pltpu.VMEM((2, 2 * BLOCK, SLOTS * BLOCK), F32),
            pltpu.VMEM((2, 2 * BLOCK, DH), F32),
            pltpu.SemaphoreType.DMA((pairs, 7)),
            pltpu.SemaphoreType.DMA((pairs,)),
        ],
        input_output_aliases={5 + len(halo): 0} if extra else {},
        compiler_params=pltpu.CompilerParams(vmem_limit_bytes=VMEM_LIMIT),
    )(index, bias, query, keys, values, *halo, *extra)


def pack_kernel(keys, values, out):
    out[0] = keys[...]
    out[1] = values[...]


def pack(keys, values, first, width):
    blocks = keys.shape[0]
    step = blocks // 2
    some = pl.BlockSpec((step, BLOCK, width), lambda i: (i, 0, first * DH // width))
    return pl.pallas_call(
        pack_kernel,
        out_shape=jax.ShapeDtypeStruct((2, blocks, BLOCK, width), BF16),
        grid=(blocks // step,),
        in_specs=[some, some],
        out_specs=pl.BlockSpec((2, step, BLOCK, width), lambda i: (0, i, 0, 0)),
    )(keys, values)


def temporal_kernel(gain_query, gain_key, tokens, *rest, first):
    out = rest[-1]
    frames, positions = tokens.shape[0], tokens.shape[1]
    rows = frames * POSITIONS
    place = lax.broadcasted_iota(jnp.int32, (rows, rows), 0) % POSITIONS
    other = lax.broadcasted_iota(jnp.int32, (rows, rows), 1) % POSITIONS
    same = place == other

    def step(number):
        where = pl.ds(number * POSITIONS, POSITIONS)
        for head in range(out.shape[2] // DH):
            channels = pl.ds(head * DH, DH)
            gains = pl.ds((first + head) * DH, DH)
            block = tokens[:, where, channels].reshape(rows, DH)
            wide = block.astype(F32)
            scaled = wide * lax.rsqrt(jnp.mean(wide * wide, axis=-1, keepdims=True) + EPSILON)
            normed_query = (scaled * gain_query[:, gains]).astype(BF16)
            normed_key = (scaled * gain_key[:, gains]).astype(BF16)
            scores = jnp.where(same, times_transposed(normed_query, normed_key), -1e30)
            largest = jnp.max(scores, axis=-1, keepdims=True)
            expo = jnp.exp2((scores - largest) * SCALE2)
            total = jnp.sum(expo, axis=-1, keepdims=True)
            result = (times(expo.astype(BF16), block) * (1.0 / total)).astype(BF16)
            mixed = (wide + result.astype(F32)).astype(BF16)
            out[:, where, channels] = mixed.reshape(frames, POSITIONS, DH)

    for number in range(positions // POSITIONS):
        step(number)


def temporal(gain_query, gain_key, tokens, source, first, width, into, total, offset):
    shape = tokens.shape[:2]
    extra = () if into is None else (into.reshape(shape + (total,)),)
    gain = pl.BlockSpec(gain_key.shape, lambda i: (0, 0))
    return pl.pallas_call(
        functools.partial(temporal_kernel, first=first),
        out_shape=jax.ShapeDtypeStruct(shape + (total,), BF16),
        grid=(1,),
        in_specs=[gain, gain, pl.BlockSpec(shape + (width,), lambda i: (0, 0, source // width))]
        + [pl.BlockSpec(memory_space=pl.ANY)] * len(extra),
        out_specs=pl.BlockSpec(shape + (width,), lambda i: (0, 0, offset // width)),
        input_output_aliases={3: 0} if extra else {},
        compiler_params=pltpu.CompilerParams(vmem_limit_bytes=VMEM_LIMIT),
    )(gain_query, gain_key, tokens, *extra)


def body(query, keys, values, key_offsets, key_counts, gain_query, gain_key):
    frame_count, stripe_rows, columns, channels = query.shape
    tokens = stripe_rows * columns
    blocks = tokens // BLOCK
    stripes, frames = lax.axis_size("rows"), lax.axis_size("frames")
    local = jnp.arange(blocks, dtype=jnp.int32)[:, None]
    target = local + key_offsets[0]
    global_block = lax.axis_index("rows") * blocks + target
    slot = jnp.arange(SLOTS, dtype=jnp.int32)[None, :]
    live = (global_block >= 0) & (global_block < stripes * blocks) & (slot < key_counts[0][:, None])
    index = target + blocks
    bias = jnp.repeat(jnp.where(live, 0.0, -1e30).astype(F32), BLOCK, axis=1)[:, None, :]
    shape = (blocks, BLOCK, channels)
    query, keys, values = query.reshape(shape), keys.reshape(shape), values.reshape(shape)
    gain_query, gain_key = gain_query[None], gain_key[None]
    middle = stripes // 2
    up = [(i, i + 1) for i in range(stripes - 1)]
    down = [(j, i) for i, j in up]
    leave = [(middle - 1, stripes - 1), (middle, 0)]
    arrive = [(stripes - 1, middle), (0, middle - 1)]

    sizes = [sum(heads for heads, _ in group) for group in GROUPS]
    firsts = [sum(sizes[:g]) for g in range(len(GROUPS))]
    halos, leaving, packs = {}, {}, {}
    for g, group in enumerate(GROUPS):
        first = firsts[g]
        for p, (heads, goes_round) in enumerate(group):
            both = pack(keys, values, first, heads * DH)
            packs[g, p] = both
            if goes_round:
                leaving[g, p] = lax.ppermute(both, "rows", leave)
                halos[g, p] = (
                    lax.ppermute(both, "rows", [p for p in up if p[0] != middle - 1]),
                    lax.ppermute(both, "rows", [p for p in down if p[0] != middle]),
                )
            else:
                halos[g, p] = (lax.ppermute(both, "rows", up), lax.ppermute(both, "rows", down))
            first += heads

    def after(value, previous):
        return value if previous is None else lax.optimization_barrier((value, previous))[0]

    def second_hops(previous):
        made = []
        for key, relayed in leaving.items():
            made.append(lax.ppermute(after(relayed, previous), "rows", arrive))
            halos[key] += (made[-1],)
        leaving.clear()
        return tuple(made)

    places = {}
    for number, pieces in enumerate(EXCHANGES):
        offset = 0
        for piece in pieces:
            places[piece] = (number, offset)
            offset += sizes[int(piece[1])] * DH
    totals = [sum(sizes[int(piece[1])] for piece in pieces) * DH for pieces in EXCHANGES]
    filled = [None] * len(EXCHANGES)
    exchanged = [None] * len(EXCHANGES)
    missing = [len(pieces) for pieces in EXCHANGES]
    previous, arrived = tuple(packs.values()), None
    for piece in KERNELS:
        g = int(piece[1])
        number, offset = places[piece]
        total = totals[number]
        if piece[0] == "F":
            first = firsts[g]
            for p, (heads, _) in enumerate(GROUPS[g]):
                filled[number] = spatial(
                    after(index, previous), bias, query, keys, values, halos[g, p], first, heads * DH, middle,
                    filled[number], total, offset,
                )
                previous = filled[number]
                first += heads
                offset += heads * DH
                if leaving and piece == HOP_AFTER:
                    arrived = second_hops(previous)
        else:
            if arrived is not None and piece == HOP_BEFORE:
                previous, arrived = (previous, arrived), None

            came, source = places["F" + piece[1]]
            filled[number] = temporal(
                after(gain_query, previous), gain_key, exchanged[came], source, firsts[g], sizes[g] * DH,
                filled[number], total, offset,
            )
            previous = filled[number]
        missing[number] -= 1
        if missing[number] == 0:
            value = filled[number].reshape(frames, tokens // frames, total)
            if number:
                value = after(value, exchanged[number - 1])
            exchanged[number] = lax.all_to_all(value, "frames", split_axis=0, concat_axis=0, tiled=True)
    outs = []
    for g, size in enumerate(sizes):
        number, offset = places["R" + str(g)]
        outs.append(exchanged[number][:, :, offset : offset + size * DH].reshape(tokens, size * DH))
    return jnp.concatenate(outs, axis=1).reshape(frame_count, stripe_rows, columns, channels)


def solution(mesh):
    placed = (
        P("frames", "rows", None, None),
        P("frames", "rows", None, None),
        P("frames", "rows", None, None),
        P("frames", "rows", None),
        P("frames", "rows"),
        P(),
        P(),
    )
    return jax.shard_map(
        body, mesh=mesh, in_specs=placed, out_specs=P("frames", "rows", None, None), check_vma=False
    )
```

```python
import functools

import jax
import jax.numpy as jnp
from jax import lax
from jax.experimental import pallas as pl
from jax.experimental.pallas import tpu as pltpu
from jax.sharding import PartitionSpec as P

DH = 128
BLOCK = 64
SLOTS = 16
CHUNK = 4
GROUPS = (((4, False),), ((4, False),), ((4, True),))
EXCHANGES = (("F0",), ("F1",), ("R0", "F2"), ("R1", "R2"))
KERNELS = ("F0", "F1", "R0", "F2", "R1", "R2")
HOP_AFTER, HOP_BEFORE = "F0", "R0"
EPSILON = 1e-06
SCALE2 = DH**-0.5 * 1.4426950408889634
POSITIONS = 32
F32 = jnp.float32
BF16 = jnp.bfloat16
UNROLL = 16
VMEM_LIMIT = 50 * 1024 * 1024


def times_transposed(a, b):
    return lax.dot_general(a, b, (((1,), (1,)), ((), ())), preferred_element_type=F32)


def times(a, b):
    return jnp.dot(a, b, preferred_element_type=F32)


def spatial_kernel(index, bias, queries, keys, values, before, after, *rest, first, offset, pairs, middle, crossing):
    crossed = rest[0] if crossing else None
    out, query, key_buf, value_buf, result, scores, maxima, sem, out_sem = rest[-9:]
    blocks = query.shape[1]
    span = CHUNK * BLOCK
    two = 2 * DH
    zeros = jnp.zeros((BLOCK, DH), BF16)

    def fetch(pair, act):
        here = pl.ds(pair * two, two)
        own = pl.ds(first * DH + pair * two, two)

        def one(source, target, number):
            act(pltpu.make_async_copy(source, target, sem.at[pair, number]))

        one(queries.at[:, :, own], query.at[pair], 0)
        for kind, (mine, target) in enumerate(((keys, key_buf), (values, value_buf))):
            one(mine.at[:, :, own], target.at[pair, pl.ds(blocks, blocks)], 1 + 3 * kind)
            for side, (source, number) in enumerate(((before, middle), (after, middle - 1))):
                place = target.at[pair, pl.ds(2 * side * blocks, blocks)]
                name = 2 + 3 * kind + side
                if not crossing:
                    one(source.at[kind, :, :, here], place, name)
                    continue
                stripe = lax.axis_index("rows")

                @pl.when(stripe == number)
                def _():
                    one(crossed.at[kind, :, :, here], place, name)

                @pl.when(stripe != number)
                def _():
                    one(source.at[kind, :, :, here], place, name)

    def chosen(buffer, pair, block, chunk):
        return jnp.concatenate([buffer[pair, index[block, CHUNK * chunk + t]] for t in range(CHUNK)], axis=0)

    def score(pair, block, slot):
        both = query[pair, block]
        stacked = jnp.concatenate(
            [
                jnp.concatenate([both[:, :DH], zeros], axis=1),
                jnp.concatenate([zeros, both[:, DH:]], axis=1),
            ],
            axis=0,
        )
        largest = None
        for chunk in range(SLOTS // CHUNK):
            place = pl.ds(chunk * span, span)
            part = times_transposed(stacked, chosen(key_buf, pair, block, chunk)) + bias[block, :, place]
            scores[slot, :, place] = part
            largest = part if largest is None else jnp.maximum(largest, part)
        largest = jnp.max(largest, axis=-1, keepdims=True)
        maxima[slot] = jnp.broadcast_to(largest, (2 * BLOCK, DH))

    def combine(pair, block, slot):
        largest = maxima[slot][:, :1]
        total, weights, picked = None, [], []
        for chunk in range(SLOTS // CHUNK):
            expo = jnp.exp2((scores[slot, :, pl.ds(chunk * span, span)] - largest) * SCALE2)
            total = expo if total is None else total + expo
            weights.append(expo.astype(BF16))
            picked.append(chosen(value_buf, pair, block, chunk))
        summed = times(jnp.concatenate(weights, axis=1), jnp.concatenate(picked, axis=0))
        inverse = 1.0 / jnp.sum(total, axis=-1, keepdims=True)
        result[pair, block, :, pl.ds(0, DH)] = (summed[:BLOCK, :DH] * inverse[:BLOCK]).astype(BF16)
        result[pair, block, :, pl.ds(DH, DH)] = (summed[BLOCK:, DH:] * inverse[BLOCK:]).astype(BF16)

    def leave(pair):
        place = pl.ds(offset + pair * two, two)
        return pltpu.make_async_copy(result.at[pair], out.at[:, :, place], out_sem.at[pair])

    for pair in range(pairs):
        fetch(pair, lambda copy: copy.start())
    for pair in range(pairs):
        fetch(pair, lambda copy: copy.wait())
        score(pair, 0, 0)

        def some_blocks(step, carry, pair=pair):
            for t in range(UNROLL):
                block = UNROLL * step + t
                score(pair, jnp.minimum(block + 1, blocks - 1), (t + 1) % 2)
                combine(pair, block, t % 2)
            return carry

        lax.fori_loop(0, blocks // UNROLL, some_blocks, 0)
        leave(pair).start()
    for pair in range(pairs):
        leave(pair).wait()


def spatial(index, bias, query, keys, values, halo, first, width, middle, into, total, offset):
    blocks = query.shape[0]
    anywhere = pl.BlockSpec(memory_space=pl.ANY)
    two = 2 * DH
    pairs = width // two
    extra = () if into is None else (into.reshape(blocks, BLOCK, total),)
    return pl.pallas_call(
        functools.partial(
            spatial_kernel, first=first, offset=offset, pairs=pairs, middle=middle, crossing=len(halo) == 3
        ),
        out_shape=jax.ShapeDtypeStruct((blocks, BLOCK, total), BF16),
        in_specs=[pl.BlockSpec(memory_space=pltpu.SMEM), pl.BlockSpec(memory_space=pltpu.VMEM)]
        + [anywhere] * (3 + len(halo) + len(extra)),
        out_specs=anywhere,
        scratch_shapes=[
            pltpu.VMEM((pairs, blocks, BLOCK, two), BF16),
            pltpu.VMEM((pairs, 3 * blocks, BLOCK, two), BF16),
            pltpu.VMEM((pairs, 3 * blocks, BLOCK, two), BF16),
            pltpu.VMEM((pairs, blocks, BLOCK, two), BF16),
            pltpu.VMEM((2, 2 * BLOCK, SLOTS * BLOCK), F32),
            pltpu.VMEM((2, 2 * BLOCK, DH), F32),
            pltpu.SemaphoreType.DMA((pairs, 7)),
            pltpu.SemaphoreType.DMA((pairs,)),
        ],
        input_output_aliases={5 + len(halo): 0} if extra else {},
        compiler_params=pltpu.CompilerParams(vmem_limit_bytes=VMEM_LIMIT),
    )(index, bias, query, keys, values, *halo, *extra)


def pack_kernel(keys, values, out):
    out[0] = keys[...]
    out[1] = values[...]


def pack(keys, values, first, width):
    blocks = keys.shape[0]
    step = blocks // 2
    some = pl.BlockSpec((step, BLOCK, width), lambda i: (i, 0, first * DH // width))
    return pl.pallas_call(
        pack_kernel,
        out_shape=jax.ShapeDtypeStruct((2, blocks, BLOCK, width), BF16),
        grid=(blocks // step,),
        in_specs=[some, some],
        out_specs=pl.BlockSpec((2, step, BLOCK, width), lambda i: (0, i, 0, 0)),
    )(keys, values)


def temporal_kernel(gain_query, gain_key, tokens, *rest, first):
    out = rest[-1]
    frames, positions = tokens.shape[0], tokens.shape[1]
    rows = frames * POSITIONS
    place = lax.broadcasted_iota(jnp.int32, (rows, rows), 0) % POSITIONS
    other = lax.broadcasted_iota(jnp.int32, (rows, rows), 1) % POSITIONS
    same = place == other

    def step(number):
        where = pl.ds(number * POSITIONS, POSITIONS)
        for head in range(out.shape[2] // DH):
            channels = pl.ds(head * DH, DH)
            gains = pl.ds((first + head) * DH, DH)
            block = tokens[:, where, channels].reshape(rows, DH)
            wide = block.astype(F32)
            scaled = wide * lax.rsqrt(jnp.mean(wide * wide, axis=-1, keepdims=True) + EPSILON)
            normed_query = (scaled * gain_query[:, gains]).astype(BF16)
            normed_key = (scaled * gain_key[:, gains]).astype(BF16)
            scores = jnp.where(same, times_transposed(normed_query, normed_key), -1e30)
            largest = jnp.max(scores, axis=-1, keepdims=True)
            expo = jnp.exp2((scores - largest) * SCALE2)
            total = jnp.sum(expo, axis=-1, keepdims=True)
            result = (times(expo.astype(BF16), block) * (1.0 / total)).astype(BF16)
            mixed = (wide + result.astype(F32)).astype(BF16)
            out[:, where, channels] = mixed.reshape(frames, POSITIONS, DH)

    for number in range(positions // POSITIONS):
        step(number)


def temporal(gain_query, gain_key, tokens, source, first, width, into, total, offset):
    shape = tokens.shape[:2]
    extra = () if into is None else (into.reshape(shape + (total,)),)
    gain = pl.BlockSpec(gain_key.shape, lambda i: (0, 0))
    return pl.pallas_call(
        functools.partial(temporal_kernel, first=first),
        out_shape=jax.ShapeDtypeStruct(shape + (total,), BF16),
        grid=(1,),
        in_specs=[gain, gain, pl.BlockSpec(shape + (width,), lambda i: (0, 0, source // width))]
        + [pl.BlockSpec(memory_space=pl.ANY)] * len(extra),
        out_specs=pl.BlockSpec(shape + (width,), lambda i: (0, 0, offset // width)),
        input_output_aliases={3: 0} if extra else {},
        compiler_params=pltpu.CompilerParams(vmem_limit_bytes=VMEM_LIMIT),
    )(gain_query, gain_key, tokens, *extra)


def body(query, keys, values, key_offsets, key_counts, gain_query, gain_key):
    frame_count, stripe_rows, columns, channels = query.shape
    tokens = stripe_rows * columns
    blocks = tokens // BLOCK
    stripes, frames = lax.axis_size("rows"), lax.axis_size("frames")
    local = jnp.arange(blocks, dtype=jnp.int32)[:, None]
    target = local + key_offsets[0]
    global_block = lax.axis_index("rows") * blocks + target
    slot = jnp.arange(SLOTS, dtype=jnp.int32)[None, :]
    live = (global_block >= 0) & (global_block < stripes * blocks) & (slot < key_counts[0][:, None])
    index = target + blocks
    bias = jnp.repeat(jnp.where(live, 0.0, -1e30).astype(F32), BLOCK, axis=1)[:, None, :]
    shape = (blocks, BLOCK, channels)
    query, keys, values = query.reshape(shape), keys.reshape(shape), values.reshape(shape)
    gain_query, gain_key = gain_query[None], gain_key[None]
    middle = stripes // 2
    up = [(i, i + 1) for i in range(stripes - 1)]
    down = [(j, i) for i, j in up]
    leave = [(middle - 1, stripes - 1), (middle, 0)]
    arrive = [(stripes - 1, middle), (0, middle - 1)]

    sizes = [sum(heads for heads, _ in group) for group in GROUPS]
    firsts = [sum(sizes[:g]) for g in range(len(GROUPS))]
    halos, leaving, packs = {}, {}, {}
    for g, group in enumerate(GROUPS):
        first = firsts[g]
        for p, (heads, goes_round) in enumerate(group):
            both = pack(keys, values, first, heads * DH)
            packs[g, p] = both
            if goes_round:
                leaving[g, p] = lax.ppermute(both, "rows", leave)
                halos[g, p] = (
                    lax.ppermute(both, "rows", [p for p in up if p[0] != middle - 1]),
                    lax.ppermute(both, "rows", [p for p in down if p[0] != middle]),
                )
            else:
                halos[g, p] = (lax.ppermute(both, "rows", up), lax.ppermute(both, "rows", down))
            first += heads

    def after(value, previous):
        return value if previous is None else lax.optimization_barrier((value, previous))[0]

    def second_hops(previous):
        made = []
        for key, relayed in leaving.items():
            made.append(lax.ppermute(after(relayed, previous), "rows", arrive))
            halos[key] += (made[-1],)
        leaving.clear()
        return tuple(made)

    places = {}
    for number, pieces in enumerate(EXCHANGES):
        offset = 0
        for piece in pieces:
            places[piece] = (number, offset)
            offset += sizes[int(piece[1])] * DH
    totals = [sum(sizes[int(piece[1])] for piece in pieces) * DH for pieces in EXCHANGES]
    filled = [None] * len(EXCHANGES)
    exchanged = [None] * len(EXCHANGES)
    missing = [len(pieces) for pieces in EXCHANGES]
    previous, arrived = tuple(packs.values()), None
    for piece in KERNELS:
        g = int(piece[1])
        number, offset = places[piece]
        total = totals[number]
        if piece[0] == "F":
            first = firsts[g]
            for p, (heads, _) in enumerate(GROUPS[g]):
                filled[number] = spatial(
                    after(index, previous), bias, query, keys, values, halos[g, p], first, heads * DH, middle,
                    filled[number], total, offset,
                )
                previous = filled[number]
                first += heads
                offset += heads * DH
                if leaving and piece == HOP_AFTER:
                    arrived = second_hops(previous)
        else:
            if arrived is not None and piece == HOP_BEFORE:
                previous, arrived = (previous, arrived), None

            came, source = places["F" + piece[1]]
            filled[number] = temporal(
                after(gain_query, previous), gain_key, exchanged[came], source, firsts[g], sizes[g] * DH,
                filled[number], total, offset,
            )
            previous = filled[number]
        missing[number] -= 1
        if missing[number] == 0:
            value = filled[number].reshape(frames, tokens // frames, total)
            if number:
                value = after(value, exchanged[number - 1])
            exchanged[number] = lax.all_to_all(value, "frames", split_axis=0, concat_axis=0, tiled=True)
    outs = []
    for g, size in enumerate(sizes):
        number, offset = places["R" + str(g)]
        outs.append(exchanged[number][:, :, offset : offset + size * DH].reshape(tokens, size * DH))
    return jnp.concatenate(outs, axis=1).reshape(frame_count, stripe_rows, columns, channels)


def solution(mesh):
    placed = (
        P("frames", "rows", None, None),
        P("frames", "rows", None, None),
        P("frames", "rows", None, None),
        P("frames", "rows", None),
        P("frames", "rows"),
        P(),
        P(),
    )
    return jax.shard_map(
        body, mesh=mesh, in_specs=placed, out_specs=P("frames", "rows", None, None), check_vma=False
    )
```
